128 devices in a mesh: dp: 16 (over x_hi, y, core), mp: 8 (over x_lo, z).
Axes of the slice: x: 4 (x_hi: 2, x_lo: 2; x = x_hi * 2 + x_lo), y: 4, z: 4, core: 2. Of those that a mesh axis runs over, the one named last changes fastest.
Arguments:
- tokens: bfloat16 [16384, 8192], P('dp', 'mp'), may hold values from -6 to 6
- w_query: bfloat16 [8192, 8192], P(None, 'mp'), may hold values from -0.0625 to 0.0625
- w_value: bfloat16 [8192, 1024], P(None, 'mp'), may hold values from -0.0625 to 0.0625
- a_both: bfloat16 [80, 8192, 128], P('dp', 'mp'), may hold values from -0.0625 to 0.0625
- b_query: bfloat16 [80, 64, 8192], P('dp', None, 'mp'), may hold values from -0.75 to 0.75
- b_value: bfloat16 [80, 64, 1024], P('dp', None, 'mp'), may hold values from -0.75 to 0.75
- request_adapter: int32 [16, 2], P('dp'), may hold values from 0 to 79
- adapter_slot: int32 [80], replicated, may hold values from 0 to 79, each once
- block_request: int32 [16, 8], P('dp'), may hold values from 0 to 1, never falling along the last dimension, each value on 1 to 7 neighbouring positions
Outputs:
- query_out: bfloat16 [16384, 8192], P('dp', 'mp')
- value_out: bfloat16 [16384, 1024], P('dp', 'mp')
The draws below stay inside these ranges and needn't reach their ends.
Inputs may be any that keep to these rules, and one draw needn't show every extreme that they name: `request_adapter`: adapter ids; several requests may name one adapter. `adapter_slot`: a permutation; the adapter stored at row s is owned by index s // 5 of dp. `block_request`: within a group never falling, every request has one block or more.
All inputs are finite; a program needn't handle non-finite values.
Results may differ from the reference program's by a relative error of at most 0.004.
Values may be sent and summed in bfloat16 or wider, within the bound.
No kernel may reach another device: no remote copies, remote signals or barrier semaphores. Data moves between devices by JAX's collectives and lax.ppermute only.
A program may use at most 192 MiB of HBM per device.

```python
import math
import jax
import jax.numpy as jnp
import numpy as np
from jax import lax

D = 8192
KV = 1024
R = 64
SEG = 128
REQ_GRP = 2
ROWS_GRP = 1024
BLK_GRP = 8
TOKENS = 16384
ADAPTERS = 80
N_DP = 16


def plant(drawn, own_key, smallest, high):
    extent = drawn.shape
    spot = [jax.random.randint(jax.random.fold_in(own_key, axis), (), 0, extent[axis]) for axis in range(len(extent))]
    drawn = drawn.at[tuple(spot)].set(smallest)
    longest = extent.index(max(extent))
    spot[longest] = (spot[longest] + 1) % extent[longest]
    return drawn.at[tuple(spot)].set(high)


def block_levels(own_key, shape, pieces, low, largest):
    factor_of, own = 1.0, jax.random.fold_in(own_key, 6)
    for axis_at, blocks in pieces:
        heights = jnp.exp(jax.random.uniform(jax.random.fold_in(own, axis_at), (blocks,), jnp.float32, low / len(pieces), largest / len(pieces)))
        factor_of = factor_of * jnp.repeat(heights, shape[axis_at] // blocks).reshape([-1 if axis == axis_at else 1 for axis in range(len(shape))])
    return factor_of


def cumulative_ranks(number_of, lean):
    portions = [(1 << 20) // math.isqrt(standing ** lean) + 1 for standing in range(1, number_of + 1)]
    deviation = 1 + sum(portions) // (1 << 30)
    return np.cumsum(np.array([max(1, weight // deviation) for weight in portions]))


def ranked_ids(own_key, extent, count, skew):
    grid = cumulative_ranks(count, skew)
    pick = jax.random.randint(jax.random.fold_in(own_key, 1), extent, 0, int(grid[count - 1]))
    grade = jnp.searchsorted(jnp.asarray(grid, jnp.int32), pick, side="right")
    return jax.random.permutation(jax.random.fold_in(own_key, 2), count)[grade].astype(jnp.int32)


def profile(number_of, total, bound, skew):
    weights = [(1 << 20) // math.isqrt(grade ** skew) + 1 for grade in range(2, number_of + 1)]
    surplus, holding = total - bound - (number_of - 1), [1] * (number_of - 1)
    while surplus > 0:
        movable = [i for i in range(number_of - 1) if holding[i] < bound]
        pool, left = sum([weights[i] for i in movable]), surplus
        for i in movable:
            extra = min(bound - holding[i], max(1, left * weights[i] // pool), surplus)
            holding[i] = holding[i] + extra
            surplus = surplus - extra
    return np.array([bound] + holding)


def uneven_parts(key, amount, total, reach, lean):
    if amount == 2:
        one = jax.random.randint(key, (), max(1, total - reach), min(reach, total - 1) + 1)
        return jnp.stack([one, total - one])
    lengths = jnp.asarray(profile(amount, total, reach, lean), jnp.int32)
    pairs = (amount - 1) // 2
    donor, sink = lengths[1:1 + 2 * pairs:2], lengths[2:2 + 2 * pairs:2]
    room = jnp.minimum(donor - 1, reach - sink)
    passed = jax.random.randint(jax.random.fold_in(key, 1), (pairs,), 0, 1 << 20) % (room + 1)
    lengths = lengths.at[1:1 + 2 * pairs:2].set(donor - passed).at[2:2 + 2 * pairs:2].set(sink + passed)
    return lengths[jax.random.permutation(jax.random.fold_in(key, 2), amount)]


def gaussian(key, extent, width, reach, shards=(), kind=jnp.bfloat16):
    drawn = width * jax.random.normal(key, extent, jnp.float32)
    if shards:
        drawn = drawn * block_levels(key, extent, shards, -0.22, 0.18)
    return jnp.clip(drawn, -reach, reach).astype(kind)


def setup_inputs(seed: int = 0) -> dict:
    keys = jax.random.split(jax.random.key(seed), 10)
    return {
        "tokens": gaussian(keys[0], (TOKENS, D), 1.0, 6.0, ((0, 16), (1, 8))),
        "w_query": gaussian(keys[1], (D, D), D ** -0.5, 0.0625, ((1, 8),)),
        "w_value": gaussian(keys[2], (D, KV), D ** -0.5, 0.0625, ((1, 8),)),
        "a_both": gaussian(keys[3], (ADAPTERS, D, 2 * R), D ** -0.5, 0.0625, ((0, 16), (1, 8))),
        "b_query": gaussian(keys[4], (ADAPTERS, R, D), R ** -0.5, 0.75, ((0, 16), (2, 8))),
        "b_value": gaussian(keys[5], (ADAPTERS, R, KV), R ** -0.5, 0.75, ((0, 16), (2, 8))),
        "request_adapter": plant(ranked_ids(keys[6], (N_DP, REQ_GRP), ADAPTERS, 2), jax.random.fold_in(keys[6], 3), 0, ADAPTERS - 1).astype(jnp.int32),
        "adapter_slot": jax.random.permutation(keys[7], ADAPTERS).astype(jnp.int32),
        "block_request": jax.vmap(lambda own: jnp.searchsorted(jnp.cumsum(uneven_parts(own, REQ_GRP, BLK_GRP, BLK_GRP - REQ_GRP + 1, 0)), jnp.arange(BLK_GRP), side="right"))(jax.random.split(keys[8], N_DP)).reshape((N_DP, BLK_GRP)).astype(jnp.int32),
    }


def reference(tokens, w_query, w_value, a_both, b_query, b_value, request_adapter, adapter_slot, block_request):
    query_parts = []
    value_parts = []
    for group in range(N_DP):
        rows = lax.dynamic_slice_in_dim(tokens, group * ROWS_GRP, ROWS_GRP, 0)
        base_query = jnp.dot(rows, w_query, preferred_element_type=jnp.float32)
        base_value = jnp.dot(rows, w_value, preferred_element_type=jnp.float32)
        row_request = jnp.repeat(block_request[group], SEG, total_repeat_length=ROWS_GRP)
        member = (row_request[:, None] == jnp.arange(REQ_GRP, dtype=jnp.int32)[None, :]).astype(jnp.float32)
        slots = [adapter_slot[request_adapter[group, r]] for r in range(REQ_GRP)]
        shrink = jnp.zeros((ROWS_GRP, 2 * R), jnp.float32)
        for r in range(REQ_GRP):
            shrink = shrink + member[:, r:r + 1] * jnp.dot(rows, a_both[slots[r]], preferred_element_type=jnp.float32)
        shrink = shrink.astype(jnp.bfloat16)
        for r in range(REQ_GRP):
            base_query = base_query + member[:, r:r + 1] * jnp.dot(shrink[:, :R], b_query[slots[r]], preferred_element_type=jnp.float32)
            base_value = base_value + member[:, r:r + 1] * jnp.dot(shrink[:, R:], b_value[slots[r]], preferred_element_type=jnp.float32)
        query_parts.append(base_query.astype(jnp.bfloat16))
        value_parts.append(base_value.astype(jnp.bfloat16))
    return jnp.concatenate(query_parts, 0), jnp.concatenate(value_parts, 0)
```

```python
import jax
import jax.numpy as jnp
from jax import lax
from jax.sharding import PartitionSpec as P

SEG = 128
NX, NZ = 2, 4
FIRST = 640


def ring_z(step):
    return [(x * NZ + z, x * NZ + (z + step) % NZ) for x in range(NX) for z in range(NZ)]


def swap_x():
    return [(i, (i + NZ) % (NX * NZ)) for i in range(NX * NZ)]


def ring_y(step):
    return [
        ((h * 4 + y) * 2 + c, (h * 4 + (y + step) % 4) * 2 + c)
        for h in range(2)
        for y in range(4)
        for c in range(2)
    ]


def swap_dp(bit):
    return [(i, i ^ bit) for i in range(16)]


def to_z(v, step):
    return lax.ppermute(v, "mp", ring_z(step))


def to_x(v):
    return lax.ppermute(v, "mp", swap_x())


def to_y(v, step):
    return lax.ppermute(v, "dp", ring_y(step))


def to_core(v):
    return lax.ppermute(v, "dp", swap_dp(1))


def to_far(v):
    return lax.ppermute(v, "dp", swap_dp(8))


def wanted_slots(request_adapter, adapter_slot):
    every = adapter_slot.shape[0]
    ids = request_adapter[0]
    slots = jnp.sum(
        jnp.where(
            ids[:, None] == jnp.arange(every, dtype=jnp.int32)[None, :], adapter_slot[None, :], 0
        ),
        axis=1,
    )
    pair = jnp.stack([slots, to_far(slots)])
    return {0: pair, 1: to_y(pair, -1), -1: to_y(pair, 1), 2: to_y(pair, 2)}


def offer(own, other, slots):
    held = own.shape[0]
    here = lax.axis_index("dp")
    picked = []
    for i in range(slots.shape[0]):
        s = slots[i]
        owner, at = s // held, s % held
        mine = lax.dynamic_index_in_dim(own, at, 0, keepdims=True)
        theirs = lax.dynamic_index_in_dim(other, at, 0, keepdims=True)
        none = jnp.zeros_like(mine)
        picked.append(
            jnp.where(owner == here, mine, jnp.where(owner == here ^ 1, theirs, none))
        )
    return jnp.concatenate(picked, axis=0)


def fetch(own, table):
    other = to_core(own)

    def part(dy, dx):
        return offer(own, other, table[dy][dx])

    near = to_y(part(2, 0), 1)
    back = to_y(part(2, 1), -1)
    up = to_y(jnp.concatenate([part(1, 0) + near, part(1, 1)]), 1)
    down = to_y(jnp.concatenate([part(-1, 0), part(-1, 1) + back]), -1)
    here = up[:2] + down[:2] + part(0, 0)
    away = up[2:] + down[2:] + part(0, 1)
    return here + to_far(away)


def reduce_rows(partial):
    rows = partial.shape[0]
    mp = lax.axis_index("mp")
    z = mp % NZ
    half = partial + to_x(partial)
    quarter = rows // NZ

    def block(step):
        return lax.dynamic_slice_in_dim(half, ((z + step) % NZ) * quarter, quarter, 0)

    total = block(0)
    for step in (1, 2, 3):
        total = total + to_z(block(step), step)
    mine = total.astype(jnp.bfloat16)
    full = jnp.zeros((rows, partial.shape[1]), jnp.bfloat16)
    full = lax.dynamic_update_slice_in_dim(full, mine, z * quarter, 0)
    for step in (1, 2, 3):
        got = to_z(mine, step)
        full = lax.dynamic_update_slice_in_dim(full, got, ((z - step) % NZ) * quarter, 0)
    return full


def on_device(
    tokens, w_query, w_value, a_both, b_query, b_value, request_adapter, adapter_slot, block_request
):
    rows, width = tokens.shape
    rank = b_query.shape[1]
    mp = lax.axis_index("mp")
    x, z = mp // NZ, mp % NZ
    half = rows // 2

    below = to_z(tokens, 1)
    above = to_z(tokens, -1)
    across = to_x(tokens)

    table = wanted_slots(request_adapter, adapter_slot)
    chosen_a = fetch(a_both, table)
    chosen_b = fetch(jnp.concatenate([b_query, b_value], axis=2), table)

    from_below = to_z(jnp.concatenate([across[:FIRST], below[:half]]), 1)
    from_above = to_z(jnp.concatenate([across[:FIRST], above[half:]]), -1)
    from_across = to_x(jnp.concatenate([below[FIRST:], above[FIRST:]]))
    rest = rows - FIRST
    opposite = jnp.concatenate([from_below[FIRST:], from_above[FIRST:]])
    across_below = jnp.concatenate([from_below[:FIRST], from_across[:rest]])
    across_above = jnp.concatenate([from_above[:FIRST], from_across[rest:]])

    cut = FIRST // 2
    last = jnp.concatenate(
        [
            to_z(from_below[:cut], 1),
            to_z(from_above[cut:FIRST], -1),
            to_x(opposite[FIRST:]),
        ]
    )

    def add(total, block, bx, step):
        at = ((x ^ bx) * NZ + (z + step) % NZ) * width
        wq = lax.dynamic_slice_in_dim(w_query, at, width, 0)
        wv = lax.dynamic_slice_in_dim(w_value, at, width, 0)
        q = jnp.dot(block, wq, preferred_element_type=jnp.float32)
        v = jnp.dot(block, wv, preferred_element_type=jnp.float32)
        return (q, v) if total is None else (total[0] + q, total[1] + v)

    total = add(None, tokens, 0, 0)
    total = add(total, below, 0, -1)
    total = add(total, above, 0, 1)
    total = add(total, across, 1, 0)
    total = add(total, opposite, 0, 2)
    total = add(total, across_below, 1, -1)
    total = add(total, across_above, 1, 1)

    row_request = jnp.repeat(block_request[0], SEG, total_repeat_length=rows)
    first = (row_request == 0)[:, None]
    both = jnp.dot(
        tokens,
        jnp.concatenate([chosen_a[0], chosen_a[1]], axis=1),
        preferred_element_type=jnp.float32,
    )
    partial = jnp.where(first, both[:, : 2 * rank], both[:, 2 * rank :])
    shrink = reduce_rows(partial)
    none = jnp.zeros_like(shrink[:, :rank])

    def spread(s):
        return jnp.concatenate([jnp.where(first, s, none), jnp.where(first, none, s)], axis=1)

    lift = chosen_b.reshape(2 * rank, -1)
    more_q = jnp.dot(
        spread(shrink[:, :rank]), lift[:, :width], preferred_element_type=jnp.float32
    )
    more_v = jnp.dot(
        spread(shrink[:, rank:]), lift[:, width:], preferred_element_type=jnp.float32
    )
    total = (total[0] + more_q, total[1] + more_v)
    total = add(total, last, 1, 2)
    return (total[0].astype(jnp.bfloat16), total[1].astype(jnp.bfloat16))


def solution(mesh):
    placed = (
        P("dp", "mp"),
        P(None, "mp"),
        P(None, "mp"),
        P("dp", "mp", None),
        P("dp", None, "mp"),
        P("dp", None, "mp"),
        P("dp", None),
        P(),
        P("dp", None),
    )
    return jax.shard_map(
        on_device,
        mesh=mesh,
        in_specs=placed,
        out_specs=(P("dp", "mp"), P("dp", "mp")),
        check_vma=False,
    )
```

```python
import functools

import jax
import jax.numpy as jnp
from jax import lax
from jax.experimental import pallas as pl
from jax.experimental.pallas import tpu as pltpu
from jax.sharding import PartitionSpec as P

SEG = 128
NX, NZ = 2, 4
TILE = 256
EARLY = 384


def pairs(move):
    found = []
    for h in range(2):
        for y in range(4):
            for c in range(2):
                for x in range(NX):
                    for z in range(NZ):
                        th, ty, tc, tx, tz = move(h, y, c, x, z, 1 - 2 * c)
                        there = ((th * 4 + ty % 4) * 2 + tc) * NX * NZ + tx * NZ + tz % NZ
                        found.append((((h * 4 + y) * 2 + c) * NX * NZ + x * NZ + z, there))
    return found


def to_z(v, step):
    return lax.ppermute(
        v, ("dp", "mp"), pairs(lambda h, y, c, x, z, s: (h, y, c, x, z + s * step))
    )


def to_y(v, step):
    return lax.ppermute(
        v, ("dp", "mp"), pairs(lambda h, y, c, x, z, s: (h, y + s * step, c, x, z))
    )


def to_x(v):
    return lax.ppermute(v, ("dp", "mp"), pairs(lambda h, y, c, x, z, s: (h, y, c, 1 - x, z)))


def to_core(v):
    return lax.ppermute(v, ("dp", "mp"), pairs(lambda h, y, c, x, z, s: (h, y, 1 - c, x, z)))


def to_far(v):
    return lax.ppermute(v, ("dp", "mp"), pairs(lambda h, y, c, x, z, s: (1 - h, y, c, x, z)))


def after(v, *earlier):
    return lax.optimization_barrier((v,) + earlier)[0]


def wanted_slots(request_adapter, adapter_slot):
    every = adapter_slot.shape[0]
    ids = request_adapter[0]
    slots = jnp.sum(
        jnp.where(
            ids[:, None] == jnp.arange(every, dtype=jnp.int32)[None, :], adapter_slot[None, :], 0
        ),
        axis=1,
    )
    far = to_far(slots)
    here = lax.axis_index("dp").astype(jnp.int32)[None]
    ends = jnp.concatenate([slots, far])
    ends = jnp.concatenate([ends, to_y(ends, 2)])
    ring = to_y(ends, 1)
    return far, jnp.concatenate([ends, here]), jnp.concatenate([ring, here])


def offer_kernel(adds, offset, held, codes, own, other, *refs):
    out = refs[-1]
    i = pl.program_id(0)
    s = codes[offset + i]
    here = codes[codes.shape[0] - 1]
    owner = s // held
    none = jnp.zeros(out.shape, out.dtype)
    value = jnp.where(owner == here, own[...], jnp.where(owner == (here ^ 1), other[...], none))
    for (start, count), ref in zip(adds, refs[:-1]):
        inside = (i >= start) & (i < start + count)
        value = value + jnp.where(inside, ref[...], none)
    out[...] = value


def offer(own, other, codes, offset, count, adds=()):
    held, block = own.shape[0], (1,) + own.shape[1:]
    last = codes.shape[0] - 1

    def stored(flip):
        def index(i, codes):
            slot = codes[offset + i]
            return (jnp.where(slot // held == codes[last] ^ flip, slot % held, 0), 0, 0)

        return pl.BlockSpec(block, index)

    in_specs = [stored(0), stored(1)]
    for _, row, start, number in adds:
        in_specs.append(
            pl.BlockSpec(
                block,
                functools.partial(
                    lambda row, start, number, i, codes: (
                        row + jnp.clip(i - start, 0, number - 1),
                        0,
                        0,
                    ),
                    row,
                    start,
                    number,
                ),
            )
        )
    size = own.size // held * own.dtype.itemsize
    return pl.pallas_call(
        functools.partial(offer_kernel, [a[2:] for a in adds], offset, held),
        grid_spec=pltpu.PrefetchScalarGridSpec(
            num_scalar_prefetch=1,
            grid=(count,),
            in_specs=in_specs,
            out_specs=pl.BlockSpec(block, lambda i, codes: (i, 0, 0)),
        ),
        out_shape=jax.ShapeDtypeStruct((count,) + own.shape[1:], own.dtype),
        compiler_params=pltpu.CompilerParams(vmem_limit_bytes=16 * 1024 * 1024),
        cost_estimate=pl.CostEstimate(
            flops=own.size, bytes_accessed=4 * count * size, transcendentals=0
        ),
    )(codes, own, other, *[a[0] for a in adds])


def matmul_kernel(pieces, with_total, final, idx, *refs):
    operands = 1 + max(p[0] for p in pieces)
    weights = 1 + max(p[4] for p in pieces)
    at = 0
    blocks = refs[at : at + operands]
    at += operands
    wq = refs[at : at + weights]
    at += weights
    wv = refs[at : at + weights]
    at += weights
    if with_total:
        tq, tv = refs[at : at + 2]
        at += 2
    if final:
        shrink, lift_q, lift_v = refs[at : at + 3]
        at += 3
    out_q, out_v = refs[at : at + 2]
    rows = out_q.shape[0]

    def spread():
        s = shrink[...]
        first = lax.broadcasted_iota(jnp.int32, s.shape, 0) < idx[weights]
        none = jnp.zeros_like(s)
        return jnp.concatenate([jnp.where(first, s, none), jnp.where(first, none, s)], axis=1)

    def run(out, ws, total, lift):
        marks = sorted({p[2] for p in pieces} | {p[2] + p[3] for p in pieces})
        more = None
        if final:
            more = jnp.dot(spread(), lift[...], preferred_element_type=jnp.float32)
        for low, high in zip(marks[:-1], marks[1:]):
            acc = None
            if with_total:
                acc = total[low:high]
            if more is not None:
                acc = acc + more[low:high]
            for op, src, dst, count, w in pieces:
                if dst <= low and high <= dst + count:
                    begin = src + low - dst
                    part = jnp.dot(
                        blocks[op][begin : begin + high - low],
                        ws[w][...],
                        preferred_element_type=jnp.float32,
                    )
                    acc = part if acc is None else acc + part
            out[low:high] = acc.astype(out.dtype)

    run(out_q, wq, tq if with_total else None, lift_q if final else None)

    @pl.when(pl.program_id(0) == 0)
    def _():
        run(out_v, wv, tv if with_total else None, lift_v if final else None)


def matmul(blocks, index, pieces, w_query, w_value, total=None, extra=None):
    weights = 1 + max(p[4] for p in pieces)
    rows = max(p[2] + p[3] for p in pieces)
    width = blocks[0].shape[1]
    nq, nv = w_query.shape[1], w_value.shape[1]
    final = extra is not None
    dtype = jnp.bfloat16 if final else jnp.float32
    whole = lambda a: pl.BlockSpec(a.shape, lambda j, idx: (0,) * a.ndim)
    in_specs = [whole(b) for b in blocks]
    in_specs += [
        pl.BlockSpec((width, TILE), functools.partial(lambda k, j, idx: (idx[k], j), k))
        for k in range(weights)
    ]
    in_specs += [
        pl.BlockSpec((width, nv), functools.partial(lambda k, j, idx: (idx[k], 0), k))
        for k in range(weights)
    ]
    operands = list(blocks) + [w_query] * weights + [w_value] * weights
    if total is not None:
        in_specs += [
            pl.BlockSpec((rows, TILE), lambda j, idx: (0, j)),
            pl.BlockSpec((rows, nv), lambda j, idx: (0, 0)),
        ]
        operands += list(total)
    if final:
        shrink, lift_q, lift_v = extra
        in_specs += [
            whole(shrink),
            pl.BlockSpec((lift_q.shape[0], TILE), lambda j, idx: (0, j)),
            whole(lift_v),
        ]
        operands += [shrink, lift_q, lift_v]
    flops = 2 * sum(p[3] for p in pieces) * width * (nq + nv)
    moved = sum(o.size * o.dtype.itemsize for o in blocks) + weights * width * (nq + nv) * 2
    moved += rows * (nq + nv) * 4 * (2 if total is not None else 1)
    return pl.pallas_call(
        functools.partial(matmul_kernel, pieces, total is not None, final),
        grid_spec=pltpu.PrefetchScalarGridSpec(
            num_scalar_prefetch=1,
            grid=(nq // TILE,),
            in_specs=in_specs,
            out_specs=[
                pl.BlockSpec((rows, TILE), lambda j, idx: (0, j)),
                pl.BlockSpec((rows, nv), lambda j, idx: (0, 0)),
            ],
        ),
        out_shape=[
            jax.ShapeDtypeStruct((rows, nq), dtype),
            jax.ShapeDtypeStruct((rows, nv), dtype),
        ],
        compiler_params=pltpu.CompilerParams(vmem_limit_bytes=44 * 1024 * 1024),
        cost_estimate=pl.CostEstimate(flops=flops, bytes_accessed=moved, transcendentals=0),
    )(index, *operands)


def shrink_kernel(bound, tokens, maps, out):
    both = jnp.concatenate([maps[0], maps[1]], axis=1)
    sums = jnp.dot(tokens[...], both, preferred_element_type=jnp.float32)
    rank = out.shape[1]
    first = lax.broadcasted_iota(jnp.int32, out.shape, 0) < bound[0]
    out[...] = jnp.where(first, sums[:, :rank], sums[:, rank:])


def partial_shrink(bound, tokens, maps):
    return pl.pallas_call(
        shrink_kernel,
        in_specs=[
            pl.BlockSpec(memory_space=pltpu.SMEM),
            pl.BlockSpec(memory_space=pltpu.VMEM),
            pl.BlockSpec(memory_space=pltpu.VMEM),
        ],
        out_specs=pl.BlockSpec(memory_space=pltpu.VMEM),
        out_shape=jax.ShapeDtypeStruct((tokens.shape[0], maps.shape[2]), jnp.float32),
        compiler_params=pltpu.CompilerParams(vmem_limit_bytes=24 * 1024 * 1024),
        cost_estimate=pl.CostEstimate(
            flops=4 * tokens.size * maps.shape[2], bytes_accessed=4 << 20, transcendentals=0
        ),
    )(bound, tokens, maps)


def on_device(
    tokens, w_query, w_value, a_both, b_query, b_value, request_adapter, adapter_slot, block_request
):
    rows, width = tokens.shape
    rank = b_query.shape[1]
    mp = lax.axis_index("mp")
    x, z = mp // NZ, mp % NZ
    s = 1 - 2 * (lax.axis_index("dp") % 2)
    bound = (SEG * jnp.sum(block_request[0] == 0)).astype(jnp.int32)

    def place(bx, step):
        return (x ^ bx) * NZ + (z + s * step) % NZ

    def add(blocks, index, pieces, total=None, extra=None):
        return matmul(blocks, index, pieces, w_query, w_value, total, extra)

    far, ends, ring = wanted_slots(request_adapter, adapter_slot)
    behind = to_z(tokens, 1)
    ahead = to_z(tokens, -1)
    across = to_x(after(tokens, far))

    other_a = to_core(a_both)
    up_message = offer(a_both, other_a, ends, 4, 2)
    up = to_y(up_message, 1)
    down_message = offer(a_both, other_a, ends, 6, 2)
    down = to_y(down_message, -1)

    own_b = jnp.concatenate([after(b_query, up_message), b_value], axis=2)
    other_b = to_core(own_b)
    total = add(
        [tokens], after(place(0, 0)[None], down_message, own_b), [(0, 0, 0, rows, 0)]
    )

    ring = after(ring, total[1], other_b)
    up_message = offer(a_both, other_a, ring, 4, 4, [(up, 0, 0, 2)])
    up = to_y(up_message, 1)
    down_message = offer(a_both, other_a, ring, 0, 4, [(down, 0, 2, 2)])
    down = to_y(down_message, -1)

    behind = after(behind, up_message, down_message)
    opposite = to_z(behind, 1)
    across = after(across, up_message, down_message)
    across_ahead = to_z(across, -1)
    cross_message = behind[:EARLY]
    cross_low = to_x(cross_message)

    far_message = offer(
        a_both, other_a, after(ends, cross_message), 2, 2, [(up, 2, 0, 2), (down, 2, 0, 2)]
    )
    far_a = to_far(far_message)
    total = add(
        [behind, ahead, across],
        after(jnp.stack([place(0, -1), place(0, 1), place(1, 0)]), far_message),
        [(k, 0, 0, rows, k) for k in range(3)],
        total,
    )

    ends_b = after(ends, total[1], cross_low)
    up_b_message = offer(own_b, other_b, ends_b, 4, 2)
    up_b = to_y(up_b_message, 1)
    down_b_message = offer(own_b, other_b, ends_b, 6, 2)
    down_b = to_y(down_b_message, -1)

    chosen_a = offer(
        a_both,
        other_a,
        after(ends, up_b_message, down_b_message),
        0,
        2,
        [(up, 0, 0, 2), (down, 0, 0, 2), (far_a, 0, 0, 2)],
    )
    narrow = lambda v: v.astype(jnp.bfloat16)
    partial = partial_shrink(bound[None], tokens, chosen_a)
    message = narrow(partial)
    partial = partial + to_x(message)
    cross_message = after(behind, message)[EARLY:]
    cross_high = to_x(cross_message)

    ring_b = after(ring, cross_message)
    up_b_message = offer(own_b, other_b, ring_b, 4, 4, [(up_b, 0, 0, 2)])
    up_b = to_y(up_b_message, 1)
    down_b_message = offer(own_b, other_b, ring_b, 0, 4, [(down_b, 0, 2, 2)])
    down_b = to_y(down_b_message, -1)

    message = narrow(after(partial, up_b_message, down_b_message))
    partial = partial + to_z(message, 1)

    last = to_z(after(across_ahead, message), -1)
    message = narrow(partial)
    shrink = narrow(partial + to_z(message, 2))
    total = add(
        [opposite, across_ahead, cross_low],
        after(jnp.stack([place(0, 2), place(1, 1), place(1, -1)]), message),
        [(0, 0, 0, rows, 0), (1, 0, 0, rows, 1), (2, 0, 0, EARLY, 2)],
        total,
    )
    far_b = to_far(
        offer(own_b, other_b, after(ends, message), 2, 2, [(up_b, 2, 0, 2), (down_b, 2, 0, 2)])
    )
    wide = offer(
        own_b, other_b, ends, 0, 2, [(up_b, 0, 0, 2), (down_b, 0, 0, 2), (far_b, 0, 0, 2)]
    )
    nq = w_query.shape[1]
    none_q = jnp.zeros((rank, nq), jnp.bfloat16)
    none_v = jnp.zeros((rank, w_value.shape[1]), jnp.bfloat16)
    lift_q = jnp.concatenate([wide[0][:, :nq], none_q, wide[1][:, :nq], none_q])
    lift_v = jnp.concatenate([none_v, wide[0][:, nq:], none_v, wide[1][:, nq:]])

    return tuple(
        add(
            [last, cross_high],
            jnp.stack([place(1, 2), place(1, -1), bound]),
            [(0, 0, 0, rows, 0), (1, 0, EARLY, rows - EARLY, 1)],
            total,
            (shrink, lift_q, lift_v),
        )
    )


def solution(mesh):
    placed = (
        P("dp", "mp"),
        P(None, "mp"),
        P(None, "mp"),
        P("dp", "mp", None),
        P("dp", None, "mp"),
        P("dp", None, "mp"),
        P("dp", None),
        P(),
        P("dp", None),
    )
    return jax.shard_map(
        on_device,
        mesh=mesh,
        in_specs=placed,
        out_specs=(P("dp", "mp"), P("dp", "mp")),
        check_vma=False,
    )
```

```python
import functools

import jax
import jax.numpy as jnp
from jax import lax
from jax.experimental import pallas as pl
from jax.experimental.pallas import tpu as pltpu
from jax.sharding import PartitionSpec as P

SEG = 128
NX, NZ = 2, 4
TILE, STEP = 512, 256
EARLY, MIDDLE = 256, 512


def pairs(move):
    found = []
    for h in range(2):
        for y in range(4):
            for c in range(2):
                for x in range(NX):
                    for z in range(NZ):
                        th, ty, tc, tx, tz = move(h, y, c, x, z, 1 - 2 * c)
                        there = ((th * 4 + ty % 4) * 2 + tc) * NX * NZ + tx * NZ + tz % NZ
                        found.append((((h * 4 + y) * 2 + c) * NX * NZ + x * NZ + z, there))
    return found


def to_z(v, step):
    return lax.ppermute(
        v, ("dp", "mp"), pairs(lambda h, y, c, x, z, s: (h, y, c, x, z + s * step))
    )


def to_y(v, step):
    return lax.ppermute(
        v, ("dp", "mp"), pairs(lambda h, y, c, x, z, s: (h, y + s * step, c, x, z))
    )


def to_x(v):
    return lax.ppermute(v, ("dp", "mp"), pairs(lambda h, y, c, x, z, s: (h, y, c, 1 - x, z)))


def to_core(v):
    return lax.ppermute(v, ("dp", "mp"), pairs(lambda h, y, c, x, z, s: (h, y, 1 - c, x, z)))


def to_far(v):
    return lax.ppermute(v, ("dp", "mp"), pairs(lambda h, y, c, x, z, s: (1 - h, y, c, x, z)))


def after(v, *earlier):
    return lax.optimization_barrier((v,) + earlier)[0]


def wanted_slots(request_adapter, adapter_slot):
    every = adapter_slot.shape[0]
    ids = request_adapter[0]
    slots = jnp.sum(
        jnp.where(
            ids[:, None] == jnp.arange(every, dtype=jnp.int32)[None, :], adapter_slot[None, :], 0
        ),
        axis=1,
    )
    far = to_far(slots)
    here = lax.axis_index("dp").astype(jnp.int32)[None]
    ends = jnp.concatenate([slots, far])
    ends = jnp.concatenate([ends, to_y(ends, 2)])
    ring = to_y(ends, 1)
    return far, jnp.concatenate([ends, here]), jnp.concatenate([ring, here])


def offer_kernel(adds, offset, count, held, codes, own, other, *refs):
    out = refs[-1]
    here = codes[codes.shape[0] - 1]
    none = jnp.zeros(out.shape[1:], out.dtype)
    for i in range(count):
        slot = codes[offset + i]
        owner, at = slot // held, slot % held
        given = [ref[row + i] for ref, (row, number) in zip(refs[:-1], adds) if i < number]
        rest = None
        for g in given:
            rest = g if rest is None else rest + g
        if rest is None:
            rest = none
        out[i] = rest

        @pl.when(owner == here)
        def _():
            out[i] = rest + own[at]

        @pl.when(owner == (here ^ 1))
        def _():
            out[i] = rest + other[at]


def offer(own, other, codes, offset, count, adds=()):
    size = own.size // own.shape[0] * own.dtype.itemsize
    vmem = pl.BlockSpec(memory_space=pltpu.VMEM)
    return pl.pallas_call(
        functools.partial(offer_kernel, [a[1:] for a in adds], offset, count, own.shape[0]),
        in_specs=[pl.BlockSpec(memory_space=pltpu.SMEM)] + [vmem] * (2 + len(adds)),
        out_specs=vmem,
        out_shape=jax.ShapeDtypeStruct((count,) + own.shape[1:], own.dtype),
        compiler_params=pltpu.CompilerParams(vmem_limit_bytes=16 * 1024 * 1024),
        cost_estimate=pl.CostEstimate(
            flops=own.size, bytes_accessed=4 * count * size, transcendentals=0
        ),
    )(codes, own, other, *[a[0] for a in adds])


def matmul_kernel(pieces, with_total, final, emit, tile, step, idx, *refs):
    operands = 1 + max(p[0] for p in pieces)
    weights = 1 + max(p[4] for p in pieces)
    refs = list(refs)
    take = lambda n: [refs.pop(0) for _ in range(n)]
    blocks = take(operands)
    w_query, w_value = take(2)
    totals = take(2) if with_total else []
    extra = take(3) if final else []
    outs = take(2)
    emitted = take(len(emit))
    held = take(operands)
    wq, wv = take(2)
    held_totals = take(2) if with_total else []
    held_extra = take(3) if final else []
    accs = take(2)
    sems, total_sems, out_sems = take(3)
    bound = idx[weights] if final else 0
    width = wq.shape[1]
    rows, nq = accs[0].shape
    copies = {}

    def fetch(name, src, dst):
        copies[name] = pltpu.make_async_copy(src, dst, sems.at[len(copies)])
        copies[name].start()

    order = []
    for p in pieces:
        if p[4] not in order:
            order.append(p[4])

    def fetch_step(n):
        for p in pieces:
            if p[4] == order[n] and ("x", p[0]) not in copies:
                fetch(("x", p[0]), blocks[p[0]], held[p[0]])
        at = pl.ds(pl.multiple_of(idx[order[n]] * width, width), width)
        fetch(("q", order[n]), w_query.at[at], wq.at[order[n]])
        fetch(("v", order[n]), w_value.at[at], wv.at[order[n]])

    for i in range(len(extra)):
        fetch(("e", i), extra[i], held_extra[i])
    fetch_step(0)

    def total_tile(j):
        at = pl.ds(pl.multiple_of(j * tile, tile), tile)
        return pltpu.make_async_copy(
            totals[0].at[:, at], held_totals[0].at[:, at], total_sems.at[j]
        )

    if with_total:
        for j in range(nq // tile):
            total_tile(j).start()
        total_value = pltpu.make_async_copy(
            totals[1], held_totals[1], total_sems.at[nq // tile]
        )
        total_value.start()
    waited = set()

    def wait(name):
        if name not in waited:
            waited.add(name)
            copies[name].wait()

    sent = []
    for n, w in enumerate(order):
        mine = [p for p in pieces if p[4] == w]
        for p in mine:
            wait(("x", p[0]))
            for i, (op, low, high) in enumerate(emit):
                if op == p[0]:
                    piece = pltpu.make_async_copy(
                        held[op].at[pl.ds(low, high - low)],
                        emitted[i],
                        out_sems.at[nq // tile + 1 + i],
                    )
                    piece.start()
                    sent.append(piece)
        wait(("q", w))
        wait(("v", w))
        last = n == len(order) - 1
        if not last:
            fetch_step(n + 1)
        if last:
            for i in range(len(extra)):
                wait(("e", i))

        def column(low, size, acc, weight, total, lift):
            for op, src, dst, count, _ in mine:
                for m in range(0, count, step):
                    mm = min(step, count - m)
                    at = pl.ds(dst + m, mm)
                    part = jnp.dot(
                        held[op][src + m : src + m + mm],
                        weight[w, :, pl.ds(low, size)],
                        preferred_element_type=jnp.float32,
                    )
                    if last and final:
                        s = held_extra[0][at]
                        row = lax.broadcasted_iota(jnp.int32, s.shape, 0) + (dst + m)
                        none = jnp.zeros_like(s)
                        s = jnp.concatenate(
                            [jnp.where(row < bound, s, none), jnp.where(row < bound, none, s)],
                            axis=1,
                        )
                        high = s.astype(jnp.bfloat16)
                        rest = (s - high.astype(jnp.float32)).astype(jnp.bfloat16)
                        for half in (high, rest):
                            part = part + jnp.dot(
                                half, lift[:, pl.ds(low, size)], preferred_element_type=jnp.float32
                            )
                    if any(
                        p[2] <= dst + m and dst + m + mm <= p[2] + p[3]
                        for p in pieces
                        if p[4] in order[:n]
                    ):
                        part = part + acc[at, pl.ds(low, size)]
                    if total is not None:
                        part = part + total[at, pl.ds(low, size)]
                    acc[at, pl.ds(low, size)] = part.astype(acc.dtype)

        nothing = (None, None)
        tq, tv = held_totals if (with_total and last) else nothing
        lq, lv = held_extra[1:] if (final and last) else nothing
        if not last:
            column(0, nq, accs[0], wq, None, None)
        else:

            @pl.loop(0, nq // tile)
            def _(j):
                low = pl.multiple_of(j * tile, tile)
                if with_total:
                    total_tile(j).wait()
                column(low, tile, accs[0], wq, tq, lq)
                at = pl.ds(low, tile)
                pltpu.make_async_copy(
                    accs[0].at[:, at], outs[0].at[:, at], out_sems.at[j]
                ).start()

            if with_total:
                total_value.wait()
        column(0, accs[1].shape[1], accs[1], wv, tv, lv)
    end = pltpu.make_async_copy(accs[1], outs[1], out_sems.at[nq // tile])
    end.start()
    for j in range(nq // tile):
        at = pl.ds(j * tile, tile)
        pltpu.make_async_copy(accs[0].at[:, at], outs[0].at[:, at], out_sems.at[j]).wait()
    end.wait()
    for piece in sent:
        piece.wait()


def matmul(blocks, index, pieces, w_query, w_value, total=None, extra=None, emit=(), tile=TILE, step=STEP):
    weights = 1 + max(p[4] for p in pieces)
    rows = max(p[2] + p[3] for p in pieces)
    width = blocks[0].shape[1]
    nq, nv = w_query.shape[1], w_value.shape[1]
    final = extra is not None
    dtype = jnp.bfloat16 if final else jnp.float32
    operands = list(blocks) + [w_query, w_value]
    scratch = [pltpu.VMEM(b.shape, b.dtype) for b in blocks]
    scratch += [pltpu.VMEM((weights, width, nq), jnp.bfloat16), pltpu.VMEM((weights, width, nv), jnp.bfloat16)]
    if total is not None:
        operands += list(total)
        scratch += [pltpu.VMEM(m.shape, m.dtype) for m in total]
    if final:
        operands += list(extra)
        scratch += [pltpu.VMEM(m.shape, m.dtype) for m in extra]
    scratch += [pltpu.VMEM((rows, nq), dtype), pltpu.VMEM((rows, nv), dtype)]
    copies = len(blocks) + 2 * weights + (3 if final else 0)
    scratch += [pltpu.SemaphoreType.DMA((copies,)), pltpu.SemaphoreType.DMA((nq // tile + 1,))]
    scratch += [pltpu.SemaphoreType.DMA((nq // tile + 1 + len(emit),))]
    hbm = pl.BlockSpec(memory_space=pltpu.HBM)
    in_specs = [hbm] * len(operands)
    flops = 2 * sum(p[3] for p in pieces) * width * (nq + nv)
    moved = sum(o.size * o.dtype.itemsize for o in blocks) + weights * width * (nq + nv) * 2
    moved += rows * (nq + nv) * 4 * (2 if total is not None else 1)
    return pl.pallas_call(
        functools.partial(matmul_kernel, pieces, total is not None, final, emit, tile, step),
        in_specs=[pl.BlockSpec(memory_space=pltpu.SMEM)] + in_specs,
        out_specs=[hbm] * (2 + len(emit)),
        out_shape=[jax.ShapeDtypeStruct((rows, nq), dtype), jax.ShapeDtypeStruct((rows, nv), dtype)]
        + [jax.ShapeDtypeStruct((high - low, width), jnp.bfloat16) for _, low, high in emit],
        scratch_shapes=scratch,
        compiler_params=pltpu.CompilerParams(vmem_limit_bytes=44 * 1024 * 1024),
        cost_estimate=pl.CostEstimate(flops=flops, bytes_accessed=moved, transcendentals=0),
    )(index, *operands)


def shrink_kernel(bound, tokens, maps, out, narrow):
    both = jnp.concatenate([maps[0], maps[1]], axis=1)
    sums = jnp.dot(tokens[...], both, preferred_element_type=jnp.float32)
    rank = out.shape[1]
    first = lax.broadcasted_iota(jnp.int32, out.shape, 0) < bound[0]
    out[...] = jnp.where(first, sums[:, :rank], sums[:, rank:])
    narrow[...] = out[...].astype(narrow.dtype)


def partial_shrink(bound, tokens, maps):
    return pl.pallas_call(
        shrink_kernel,
        in_specs=[
            pl.BlockSpec(memory_space=pltpu.SMEM),
            pl.BlockSpec(memory_space=pltpu.VMEM),
            pl.BlockSpec(memory_space=pltpu.VMEM),
        ],
        out_specs=[pl.BlockSpec(memory_space=pltpu.VMEM)] * 2,
        out_shape=[
            jax.ShapeDtypeStruct((tokens.shape[0], maps.shape[2]), jnp.float32),
            jax.ShapeDtypeStruct((tokens.shape[0], maps.shape[2]), jnp.bfloat16),
        ],
        compiler_params=pltpu.CompilerParams(vmem_limit_bytes=24 * 1024 * 1024),
        cost_estimate=pl.CostEstimate(
            flops=4 * tokens.size * maps.shape[2], bytes_accessed=4 << 20, transcendentals=0
        ),
    )(bound, tokens, maps)


def on_device(
    tokens, w_query, w_value, a_both, b_query, b_value, request_adapter, adapter_slot, block_request
):
    rows, width = tokens.shape
    rank = b_query.shape[1]
    mp = lax.axis_index("mp")
    x, z = mp // NZ, mp % NZ
    s = 1 - 2 * (lax.axis_index("dp") % 2)
    bound = (SEG * jnp.sum(block_request[0] == 0)).astype(jnp.int32)

    def place(bx, step):
        return (x ^ bx) * NZ + (z + s * step) % NZ

    def add(blocks, index, pieces, total=None, extra=None, emit=()):
        return matmul(blocks, index, pieces, w_query, w_value, total, extra, emit)

    far, ends, ring = wanted_slots(request_adapter, adapter_slot)
    behind = to_z(tokens, 1)
    ahead = to_z(tokens, -1)
    across = to_x(after(tokens, far))

    other_a = to_core(a_both)
    message = offer(a_both, other_a, after(ends, ring), 4, 4)
    up = to_y(message, 1)
    own_b = jnp.concatenate([after(b_query, message), b_value], axis=2)
    other_b = to_core(own_b)
    total = add([tokens], after(place(0, 0)[None], message, own_b), [(0, 0, 0, rows, 0)])

    ring = after(ring, total[1], other_b)
    down_message = offer(a_both, other_a, ring, 0, 4)
    down = to_y(down_message, -1)
    up_message = offer(a_both, other_a, after(ring, down_message), 4, 4, [(up, 0, 4)])
    up = to_y(up_message, 1)
    first_b_message = offer(own_b, other_b, after(ends, up_message), 4, 4)
    down_b_message = offer(own_b, other_b, after(ring, first_b_message), 0, 4)

    behind = after(behind, down_b_message)
    opposite = to_z(behind, 1)
    cross_message = behind[:EARLY]
    cross_low = to_x(cross_message)
    across = after(across, cross_message)
    across_ahead = to_z(across, -1)

    *total, middle_message, high_message = add(
        [behind],
        after(place(0, -1)[None], cross_message),
        [(0, 0, 0, rows, 0)],
        total,
        emit=((0, EARLY, MIDDLE), (0, MIDDLE, rows)),
    )
    far_message = offer(a_both, other_a, after(ends, total[1]), 2, 2, [(up, 2, 2), (down, 2, 2)])
    far_a = to_far(far_message)
    message = after(first_b_message, far_message)
    up_b = to_y(message, 1)
    total = add(
        [ahead, across],
        after(jnp.stack([place(0, 1), place(1, 0)]), message),
        [(k, 0, 0, rows, k) for k in range(2)],
        total,
    )
    cross_message = after(middle_message, total[1], cross_low)
    cross_middle = to_x(cross_message)
    ends = after(ends, cross_message)

    chosen_a = offer(
        a_both,
        other_a,
        ends,
        0,
        2,
        [(up, 0, 2), (down, 0, 2), (far_a, 0, 2)],
    )
    narrow = lambda v: v.astype(jnp.bfloat16)
    partial, message = partial_shrink(bound[None], tokens, chosen_a)
    half = partial + to_x(message)
    down_b_message = after(down_b_message, message, far_a)
    down_b = to_y(down_b_message, -1)
    ring_b = after(ring, down_b_message)
    up_b_message = offer(own_b, other_b, ring_b, 4, 4, [(up_b, 0, 4)])
    up_b = to_y(up_b_message, 1)

    last_message = after(across_ahead, up_b_message, opposite)
    last = to_z(last_message, -1)
    cross_message = after(high_message, message, cross_middle)
    cross_high = to_x(cross_message)
    message = narrow(half)
    pair = half + to_z(message, 1)
    total = add(
        [opposite],
        after(place(0, 2)[None], cross_message, message),
        [(0, 0, 0, rows, 0)],
        total,
    )
    message = after(narrow(pair), total[1])
    shrink = pair + to_z(message, 2)
    far_b = to_far(
        offer(own_b, other_b, after(ends, message, cross_high), 2, 2, [(up_b, 2, 2), (down_b, 2, 2)])
    )
    total = add(
        [cross_low, cross_middle, across_ahead],
        after(jnp.stack([place(1, -1), place(1, 1)]), message),
        [
            (0, 0, 0, EARLY, 0),
            (1, 0, EARLY, MIDDLE - EARLY, 0),
            (2, 0, 0, rows, 1),
        ],
        total,
    )
    ends = after(ends, total[1])
    wide = offer(
        own_b, other_b, ends, 0, 2, [(up_b, 0, 2), (down_b, 0, 2), (far_b, 0, 2)]
    )
    nq = w_query.shape[1]
    none_q = jnp.zeros((rank, nq), jnp.bfloat16)
    none_v = jnp.zeros((rank, w_value.shape[1]), jnp.bfloat16)
    lift_q = jnp.concatenate([wide[0][:, :nq], none_q, wide[1][:, :nq], none_q])
    lift_v = jnp.concatenate([none_v, wide[0][:, nq:], none_v, wide[1][:, nq:]])

    return tuple(
        add(
            [cross_high, last],
            jnp.stack([place(1, -1), place(1, 2), bound]),
            [(0, 0, MIDDLE, rows - MIDDLE, 0), (1, 0, 0, rows, 1)],
            total,
            (shrink, lift_q, lift_v),
        )
    )


def solution(mesh):
    placed = (
        P("dp", "mp"),
        P(None, "mp"),
        P(None, "mp"),
        P("dp", "mp", None),
        P("dp", None, "mp"),
        P("dp", None, "mp"),
        P("dp", None),
        P(),
        P("dp", None),
    )
    return jax.shard_map(
        on_device,
        mesh=mesh,
        in_specs=placed,
        out_specs=(P("dp", "mp"), P("dp", "mp")),
        check_vma=False,
    )
```

```python
import functools

import jax
import jax.numpy as jnp
from jax import lax
from jax.experimental import pallas as pl
from jax.experimental.pallas import tpu as pltpu
from jax.sharding import PartitionSpec as P

SEG = 128
NX, NZ = 2, 4
TILE, STEP = 512, 256
EARLY, MIDDLE = 256, 512


def pairs(move):
    found = []
    for h in range(2):
        for y in range(4):
            for c in range(2):
                for x in range(NX):
                    for z in range(NZ):
                        th, ty, tc, tx, tz = move(h, y, c, x, z, 1 - 2 * c)
                        there = ((th * 4 + ty % 4) * 2 + tc) * NX * NZ + tx * NZ + tz % NZ
                        found.append((((h * 4 + y) * 2 + c) * NX * NZ + x * NZ + z, there))
    return found


def to_z(v, step):
    return lax.ppermute(
        v, ("dp", "mp"), pairs(lambda h, y, c, x, z, s: (h, y, c, x, z + s * step))
    )


def to_y(v, step):
    return lax.ppermute(
        v, ("dp", "mp"), pairs(lambda h, y, c, x, z, s: (h, y + s * step, c, x, z))
    )


def to_x(v):
    return lax.ppermute(v, ("dp", "mp"), pairs(lambda h, y, c, x, z, s: (h, y, c, 1 - x, z)))


def to_core(v):
    return lax.ppermute(v, ("dp", "mp"), pairs(lambda h, y, c, x, z, s: (h, y, 1 - c, x, z)))


def to_far(v):
    return lax.ppermute(v, ("dp", "mp"), pairs(lambda h, y, c, x, z, s: (1 - h, y, c, x, z)))


def after(v, *earlier):
    return lax.optimization_barrier((v,) + earlier)[0]


def wanted_slots(request_adapter, adapter_slot):
    every = adapter_slot.shape[0]
    ids = request_adapter[0]
    slots = jnp.sum(
        jnp.where(
            ids[:, None] == jnp.arange(every, dtype=jnp.int32)[None, :], adapter_slot[None, :], 0
        ),
        axis=1,
    )
    far = to_far(slots)
    here = lax.axis_index("dp").astype(jnp.int32)[None]
    ends = jnp.concatenate([slots, far])
    ends = jnp.concatenate([ends, to_y(ends, 2)])
    ring = to_y(ends, 1)
    return far, jnp.concatenate([ends, here]), jnp.concatenate([ring, here])


def offer_kernel(adds, offset, count, held, codes, own, other, *refs):
    out = refs[-1]
    here = codes[codes.shape[0] - 1]
    none = jnp.zeros(out.shape[1:], out.dtype)
    for i in range(count):
        slot = codes[offset + i]
        owner, at = slot // held, slot % held
        given = [ref[row + i] for ref, (row, number) in zip(refs[:-1], adds) if i < number]
        rest = None
        for g in given:
            rest = g if rest is None else rest + g
        if rest is None:
            rest = none
        out[i] = rest

        @pl.when(owner == here)
        def _():
            out[i] = rest + own[at]

        @pl.when(owner == (here ^ 1))
        def _():
            out[i] = rest + other[at]


def offer(own, other, codes, offset, count, adds=()):
    size = own.size // own.shape[0] * own.dtype.itemsize
    vmem = pl.BlockSpec(memory_space=pltpu.VMEM)
    return pl.pallas_call(
        functools.partial(offer_kernel, [a[1:] for a in adds], offset, count, own.shape[0]),
        in_specs=[pl.BlockSpec(memory_space=pltpu.SMEM)] + [vmem] * (2 + len(adds)),
        out_specs=vmem,
        out_shape=jax.ShapeDtypeStruct((count,) + own.shape[1:], own.dtype),
        compiler_params=pltpu.CompilerParams(vmem_limit_bytes=16 * 1024 * 1024),
        cost_estimate=pl.CostEstimate(
            flops=own.size, bytes_accessed=4 * count * size, transcendentals=0
        ),
    )(codes, own, other, *[a[0] for a in adds])


def matmul_kernel(pieces, with_total, final, emit, tile, step, idx, *refs):
    operands = 1 + max(p[0] for p in pieces)
    weights = 1 + max(p[4] for p in pieces)
    refs = list(refs)
    take = lambda n: [refs.pop(0) for _ in range(n)]
    blocks = take(operands)
    w_query, w_value = take(2)
    totals = take(2) if with_total else []
    extra = take(4) if final else []
    outs = take(2)
    emitted = take(len(emit))
    held = take(operands)
    wq, wv = take(2)
    held_totals = take(2) if with_total else []
    held_extra = take(4) if final else []
    accs = take(2)
    sems, total_sems, out_sems = take(3)
    bound = idx[weights] if final else 0
    width = wq.shape[1]
    rows, nq = accs[0].shape
    copies = {}

    def fetch(name, src, dst):
        copies[name] = pltpu.make_async_copy(src, dst, sems.at[len(copies)])
        copies[name].start()

    order = []
    for p in pieces:
        if p[4] not in order:
            order.append(p[4])

    def fetch_step(n):
        for p in pieces:
            if p[4] == order[n] and ("x", p[0]) not in copies:
                fetch(("x", p[0]), blocks[p[0]], held[p[0]])
        at = pl.ds(pl.multiple_of(idx[order[n]] * width, width), width)
        fetch(("q", order[n]), w_query.at[at], wq.at[order[n]])
        fetch(("v", order[n]), w_value.at[at], wv.at[order[n]])

    for i in range(len(extra)):
        fetch(("e", i), extra[i], held_extra[i])
    fetch_step(0)

    def total_tile(j):
        at = pl.ds(pl.multiple_of(j * tile, tile), tile)
        return pltpu.make_async_copy(
            totals[0].at[:, at], held_totals[0].at[:, at], total_sems.at[j]
        )

    if with_total:
        for j in range(nq // tile):
            total_tile(j).start()
        total_value = pltpu.make_async_copy(
            totals[1], held_totals[1], total_sems.at[nq // tile]
        )
        total_value.start()
    waited = set()

    def wait(name):
        if name not in waited:
            waited.add(name)
            copies[name].wait()

    sent = []
    for n, w in enumerate(order):
        mine = [p for p in pieces if p[4] == w]
        for p in mine:
            wait(("x", p[0]))
            for i, (op, low, high) in enumerate(emit):
                if op == p[0]:
                    piece = pltpu.make_async_copy(
                        held[op].at[pl.ds(low, high - low)],
                        emitted[i],
                        out_sems.at[nq // tile + 1 + i],
                    )
                    piece.start()
                    sent.append(piece)
        wait(("q", w))
        wait(("v", w))
        last = n == len(order) - 1
        if not last:
            fetch_step(n + 1)
        if last:
            for i in range(len(extra)):
                wait(("e", i))

        def column(low, size, acc, weight, total, lift):
            for op, src, dst, count, _ in mine:
                for m in range(0, count, step):
                    mm = min(step, count - m)
                    at = pl.ds(dst + m, mm)
                    part = jnp.dot(
                        held[op][src + m : src + m + mm],
                        weight[w, :, pl.ds(low, size)],
                        preferred_element_type=jnp.float32,
                    )
                    if last and final:
                        s = held_extra[0][at] + held_extra[1][at].astype(jnp.float32)
                        row = lax.broadcasted_iota(jnp.int32, s.shape, 0) + (dst + m)
                        none = jnp.zeros_like(s)
                        s = jnp.concatenate(
                            [jnp.where(row < bound, s, none), jnp.where(row < bound, none, s)],
                            axis=1,
                        )
                        high = s.astype(jnp.bfloat16)
                        rest = (s - high.astype(jnp.float32)).astype(jnp.bfloat16)
                        for half in (high, rest):
                            part = part + jnp.dot(
                                half, lift[:, pl.ds(low, size)], preferred_element_type=jnp.float32
                            )
                    if any(
                        p[2] <= dst + m and dst + m + mm <= p[2] + p[3]
                        for p in pieces
                        if p[4] in order[:n]
                    ):
                        part = part + acc[at, pl.ds(low, size)]
                    if total is not None:
                        part = part + total[at, pl.ds(low, size)]
                    acc[at, pl.ds(low, size)] = part.astype(acc.dtype)

        nothing = (None, None)
        tq, tv = held_totals if (with_total and last) else nothing
        lq, lv = held_extra[2:] if (final and last) else nothing
        if not last:
            column(0, nq, accs[0], wq, None, None)
        else:

            @pl.loop(0, nq // tile)
            def _(j):
                low = pl.multiple_of(j * tile, tile)
                if with_total:
                    total_tile(j).wait()
                column(low, tile, accs[0], wq, tq, lq)
                at = pl.ds(low, tile)
                pltpu.make_async_copy(
                    accs[0].at[:, at], outs[0].at[:, at], out_sems.at[j]
                ).start()

            if with_total:
                total_value.wait()
        column(0, accs[1].shape[1], accs[1], wv, tv, lv)
    end = pltpu.make_async_copy(accs[1], outs[1], out_sems.at[nq // tile])
    end.start()
    for j in range(nq // tile):
        at = pl.ds(j * tile, tile)
        pltpu.make_async_copy(accs[0].at[:, at], outs[0].at[:, at], out_sems.at[j]).wait()
    end.wait()
    for piece in sent:
        piece.wait()


def matmul(blocks, index, pieces, w_query, w_value, total=None, extra=None, emit=(), tile=TILE, step=STEP):
    weights = 1 + max(p[4] for p in pieces)
    rows = max(p[2] + p[3] for p in pieces)
    width = blocks[0].shape[1]
    nq, nv = w_query.shape[1], w_value.shape[1]
    final = extra is not None
    dtype = jnp.bfloat16 if final else jnp.float32
    operands = list(blocks) + [w_query, w_value]
    scratch = [pltpu.VMEM(b.shape, b.dtype) for b in blocks]
    scratch += [pltpu.VMEM((weights, width, nq), jnp.bfloat16), pltpu.VMEM((weights, width, nv), jnp.bfloat16)]
    if total is not None:
        operands += list(total)
        scratch += [pltpu.VMEM(m.shape, m.dtype) for m in total]
    if final:
        operands += list(extra)
        scratch += [pltpu.VMEM(m.shape, m.dtype) for m in extra]
    scratch += [pltpu.VMEM((rows, nq), dtype), pltpu.VMEM((rows, nv), dtype)]
    copies = len(blocks) + 2 * weights + (4 if final else 0)
    scratch += [pltpu.SemaphoreType.DMA((copies,)), pltpu.SemaphoreType.DMA((nq // tile + 1,))]
    scratch += [pltpu.SemaphoreType.DMA((nq // tile + 1 + len(emit),))]
    hbm = pl.BlockSpec(memory_space=pltpu.HBM)
    in_specs = [hbm] * len(operands)
    flops = 2 * sum(p[3] for p in pieces) * width * (nq + nv)
    moved = sum(o.size * o.dtype.itemsize for o in blocks) + weights * width * (nq + nv) * 2
    moved += rows * (nq + nv) * 4 * (2 if total is not None else 1)
    return pl.pallas_call(
        functools.partial(matmul_kernel, pieces, total is not None, final, emit, tile, step),
        in_specs=[pl.BlockSpec(memory_space=pltpu.SMEM)] + in_specs,
        out_specs=[hbm] * (2 + len(emit)),
        out_shape=[jax.ShapeDtypeStruct((rows, nq), dtype), jax.ShapeDtypeStruct((rows, nv), dtype)]
        + [jax.ShapeDtypeStruct((high - low, width), jnp.bfloat16) for _, low, high in emit],
        scratch_shapes=scratch,
        compiler_params=pltpu.CompilerParams(vmem_limit_bytes=44 * 1024 * 1024),
        cost_estimate=pl.CostEstimate(flops=flops, bytes_accessed=moved, transcendentals=0),
    )(index, *operands)


def shrink_kernel(bound, tokens, maps, out, narrow):
    both = jnp.concatenate([maps[0], maps[1]], axis=1)
    sums = jnp.dot(tokens[...], both, preferred_element_type=jnp.float32)
    rank = out.shape[1]
    first = lax.broadcasted_iota(jnp.int32, out.shape, 0) < bound[0]
    out[...] = jnp.where(first, sums[:, :rank], sums[:, rank:])
    narrow[...] = out[...].astype(narrow.dtype)


def partial_shrink(bound, tokens, maps):
    return pl.pallas_call(
        shrink_kernel,
        in_specs=[
            pl.BlockSpec(memory_space=pltpu.SMEM),
            pl.BlockSpec(memory_space=pltpu.VMEM),
            pl.BlockSpec(memory_space=pltpu.VMEM),
        ],
        out_specs=[pl.BlockSpec(memory_space=pltpu.VMEM)] * 2,
        out_shape=[
            jax.ShapeDtypeStruct((tokens.shape[0], maps.shape[2]), jnp.float32),
            jax.ShapeDtypeStruct((tokens.shape[0], maps.shape[2]), jnp.bfloat16),
        ],
        compiler_params=pltpu.CompilerParams(vmem_limit_bytes=24 * 1024 * 1024),
        cost_estimate=pl.CostEstimate(
            flops=4 * tokens.size * maps.shape[2], bytes_accessed=4 << 20, transcendentals=0
        ),
    )(bound, tokens, maps)


def on_device(
    tokens, w_query, w_value, a_both, b_query, b_value, request_adapter, adapter_slot, block_request
):
    rows, width = tokens.shape
    rank = b_query.shape[1]
    mp = lax.axis_index("mp")
    x, z = mp // NZ, mp % NZ
    s = 1 - 2 * (lax.axis_index("dp") % 2)
    bound = (SEG * jnp.sum(block_request[0] == 0)).astype(jnp.int32)

    def place(bx, step):
        return (x ^ bx) * NZ + (z + s * step) % NZ

    def add(blocks, index, pieces, total=None, extra=None, emit=()):
        return matmul(blocks, index, pieces, w_query, w_value, total, extra, emit)

    far, ends, ring = wanted_slots(request_adapter, adapter_slot)
    behind = to_z(tokens, 1)
    ahead = to_z(tokens, -1)
    across = to_x(after(tokens, far))

    other_a = to_core(a_both)
    message = offer(a_both, other_a, after(ends, ring), 4, 4)
    up = to_y(message, 1)
    own_b = jnp.concatenate([after(b_query, message), b_value], axis=2)
    other_b = to_core(own_b)
    total = add([tokens], after(place(0, 0)[None], message, own_b), [(0, 0, 0, rows, 0)])

    ring = after(ring, total[1], other_b)
    down_message = offer(a_both, other_a, ring, 0, 4)
    down = to_y(down_message, -1)
    up_message = offer(a_both, other_a, after(ring, down_message), 4, 4, [(up, 0, 4)])
    up = to_y(up_message, 1)
    first_b_message = offer(own_b, other_b, after(ends, up_message), 4, 4)
    down_b_message = offer(own_b, other_b, after(ring, first_b_message), 0, 4)

    behind = after(behind, down_b_message)
    opposite = to_z(behind, 1)
    cross_message = behind[:EARLY]
    cross_low = to_x(cross_message)
    across = after(across, cross_message)
    across_ahead = to_z(across, -1)

    *total, middle_message, high_message = add(
        [behind],
        after(place(0, -1)[None], cross_message),
        [(0, 0, 0, rows, 0)],
        total,
        emit=((0, EARLY, MIDDLE), (0, MIDDLE, rows)),
    )
    far_message = offer(a_both, other_a, after(ends, total[1]), 2, 2, [(up, 2, 2), (down, 2, 2)])
    far_a = to_far(far_message)
    message = after(first_b_message, far_message)
    up_b = to_y(message, 1)
    total = add(
        [ahead, across],
        after(jnp.stack([place(0, 1), place(1, 0)]), message),
        [(k, 0, 0, rows, k) for k in range(2)],
        total,
    )
    cross_message = after(middle_message, total[1], cross_low)
    cross_middle = to_x(cross_message)
    ends = after(ends, cross_message)

    chosen_a = offer(
        a_both,
        other_a,
        ends,
        0,
        2,
        [(up, 0, 2), (down, 0, 2), (far_a, 0, 2)],
    )
    narrow = lambda v: v.astype(jnp.bfloat16)
    partial, message = partial_shrink(bound[None], tokens, chosen_a)
    half = partial + to_x(message)
    down_b_message = after(down_b_message, message, far_a)
    down_b = to_y(down_b_message, -1)
    ring_b = after(ring, down_b_message)
    up_b_message = offer(own_b, other_b, ring_b, 4, 4, [(up_b, 0, 4)])
    up_b = to_y(up_b_message, 1)

    last_message = after(across_ahead, up_b_message, opposite)
    last = to_z(last_message, -1)
    cross_message = after(high_message, message, cross_middle)
    cross_high = to_x(cross_message)
    message = narrow(half)
    pair = half + to_z(message, 1)
    total = add(
        [opposite],
        after(place(0, 2)[None], cross_message, message),
        [(0, 0, 0, rows, 0)],
        total,
    )
    message = after(narrow(pair), total[1])
    pair_opposite = to_z(message, 2)
    far_b = to_far(
        offer(own_b, other_b, after(ends, message, cross_high), 2, 2, [(up_b, 2, 2), (down_b, 2, 2)])
    )
    total = add(
        [cross_low, cross_middle, cross_high, across_ahead],
        after(jnp.stack([place(1, -1), place(1, 1)]), message),
        [
            (0, 0, 0, EARLY, 0),
            (1, 0, EARLY, MIDDLE - EARLY, 0),
            (2, 0, MIDDLE, rows - MIDDLE, 0),
            (3, 0, 0, rows, 1),
        ],
        total,
    )
    ends = after(ends, total[1])
    wide = offer(
        own_b, other_b, ends, 0, 2, [(up_b, 0, 2), (down_b, 0, 2), (far_b, 0, 2)]
    )
    nq = w_query.shape[1]
    none_q = jnp.zeros((rank, nq), jnp.bfloat16)
    none_v = jnp.zeros((rank, w_value.shape[1]), jnp.bfloat16)
    lift_q = jnp.concatenate([wide[0][:, :nq], none_q, wide[1][:, :nq], none_q])
    lift_v = jnp.concatenate([none_v, wide[0][:, nq:], none_v, wide[1][:, nq:]])

    return tuple(
        add(
            [last],
            jnp.stack([place(1, 2), bound]),
            [(0, 0, 0, rows, 0)],
            total,
            (pair, pair_opposite, lift_q, lift_v),
        )
    )


def solution(mesh):
    placed = (
        P("dp", "mp"),
        P(None, "mp"),
        P(None, "mp"),
        P("dp", "mp", None),
        P("dp", None, "mp"),
        P("dp", None, "mp"),
        P("dp", None),
        P(),
        P("dp", None),
    )
    return jax.shard_map(
        on_device,
        mesh=mesh,
        in_specs=placed,
        out_specs=(P("dp", "mp"), P("dp", "mp")),
        check_vma=False,
    )
```

```python
import functools

import jax
import jax.numpy as jnp
from jax import lax
from jax.experimental import pallas as pl
from jax.experimental.pallas import tpu as pltpu
from jax.sharding import PartitionSpec as P

SEG = 128
NX, NZ = 2, 4
TILE, STEP = 512, 256
EARLY, MIDDLE = 256, 512


def pairs(move):
    found = []
    for h in range(2):
        for y in range(4):
            for c in range(2):
                for x in range(NX):
                    for z in range(NZ):
                        th, ty, tc, tx, tz = move(h, y, c, x, z, 1 - 2 * c)
                        there = ((th * 4 + ty % 4) * 2 + tc) * NX * NZ + tx * NZ + tz % NZ
                        found.append((((h * 4 + y) * 2 + c) * NX * NZ + x * NZ + z, there))
    return found


def to_z(v, step):
    return lax.ppermute(
        v, ("dp", "mp"), pairs(lambda h, y, c, x, z, s: (h, y, c, x, z + s * step))
    )


def to_y(v, step):
    return lax.ppermute(
        v, ("dp", "mp"), pairs(lambda h, y, c, x, z, s: (h, y + s * step, c, x, z))
    )


def to_x(v):
    return lax.ppermute(v, ("dp", "mp"), pairs(lambda h, y, c, x, z, s: (h, y, c, 1 - x, z)))


def to_core(v):
    return lax.ppermute(v, ("dp", "mp"), pairs(lambda h, y, c, x, z, s: (h, y, 1 - c, x, z)))


def to_far(v):
    return lax.ppermute(v, ("dp", "mp"), pairs(lambda h, y, c, x, z, s: (1 - h, y, c, x, z)))


def after(v, *earlier):
    return lax.optimization_barrier((v,) + earlier)[0]


def wanted_slots(request_adapter, adapter_slot):
    every = adapter_slot.shape[0]
    ids = request_adapter[0]
    slots = jnp.sum(
        jnp.where(
            ids[:, None] == jnp.arange(every, dtype=jnp.int32)[None, :], adapter_slot[None, :], 0
        ),
        axis=1,
    )
    far = to_far(slots)
    here = lax.axis_index("dp").astype(jnp.int32)[None]
    ends = jnp.concatenate([slots, far])
    ends = jnp.concatenate([ends, to_y(ends, 2)])
    ring = to_y(ends, 1)
    return far, jnp.concatenate([ends, here]), jnp.concatenate([ring, here])


def offer_kernel(adds, offset, count, held, codes, own, other, *refs):
    out = refs[-1]
    here = codes[codes.shape[0] - 1]
    none = jnp.zeros(out.shape[1:], out.dtype)
    for i in range(count):
        slot = codes[offset + i]
        owner, at = slot // held, slot % held
        given = [ref[row + i] for ref, (row, number) in zip(refs[:-1], adds) if i < number]
        rest = None
        for g in given:
            rest = g if rest is None else rest + g
        if rest is None:
            rest = none
        out[i] = rest

        @pl.when(owner == here)
        def _():
            out[i] = rest + own[at]

        @pl.when(owner == (here ^ 1))
        def _():
            out[i] = rest + other[at]


def offer(own, other, codes, offset, count, adds=()):
    size = own.size // own.shape[0] * own.dtype.itemsize
    vmem = pl.BlockSpec(memory_space=pltpu.VMEM)
    return pl.pallas_call(
        functools.partial(offer_kernel, [a[1:] for a in adds], offset, count, own.shape[0]),
        in_specs=[pl.BlockSpec(memory_space=pltpu.SMEM)] + [vmem] * (2 + len(adds)),
        out_specs=vmem,
        out_shape=jax.ShapeDtypeStruct((count,) + own.shape[1:], own.dtype),
        compiler_params=pltpu.CompilerParams(vmem_limit_bytes=16 * 1024 * 1024),
        cost_estimate=pl.CostEstimate(
            flops=own.size, bytes_accessed=4 * count * size, transcendentals=0
        ),
    )(codes, own, other, *[a[0] for a in adds])


def matmul_kernel(pieces, with_total, final, emit, tile, step, idx, *refs):
    operands = 1 + max(p[0] for p in pieces)
    weights = 1 + max(p[4] for p in pieces)
    refs = list(refs)
    take = lambda n: [refs.pop(0) for _ in range(n)]
    blocks = take(operands)
    w_query, w_value = take(2)
    totals = take(2) if with_total else []
    extra = take(4) if final else []
    outs = take(2)
    emitted = take(len(emit))
    held = take(operands)
    wq, wv = take(2)
    held_totals = take(2) if with_total else []
    held_extra = take(4) if final else []
    accs = take(2)
    sems, total_sems, out_sems = take(3)
    bound = idx[weights] if final else 0
    width = wq.shape[1]
    rows, nq = accs[0].shape
    copies = {}

    def fetch(name, src, dst):
        copies[name] = pltpu.make_async_copy(src, dst, sems.at[len(copies)])
        copies[name].start()

    order = []
    for p in pieces:
        if p[4] not in order:
            order.append(p[4])

    def fetch_step(n):
        for p in pieces:
            if p[4] == order[n] and ("x", p[0]) not in copies:
                fetch(("x", p[0]), blocks[p[0]], held[p[0]])
        at = pl.ds(pl.multiple_of(idx[order[n]] * width, width), width)
        fetch(("q", order[n]), w_query.at[at], wq.at[order[n]])
        fetch(("v", order[n]), w_value.at[at], wv.at[order[n]])

    for i in range(len(extra)):
        fetch(("e", i), extra[i], held_extra[i])
    fetch_step(0)

    def total_tile(j):
        at = pl.ds(pl.multiple_of(j * tile, tile), tile)
        return pltpu.make_async_copy(
            totals[0].at[:, at], held_totals[0].at[:, at], total_sems.at[j]
        )

    if with_total:
        for j in range(nq // tile):
            total_tile(j).start()
        total_value = pltpu.make_async_copy(
            totals[1], held_totals[1], total_sems.at[nq // tile]
        )
        total_value.start()
    waited = set()

    def wait(name):
        if name not in waited:
            waited.add(name)
            copies[name].wait()

    sent = []
    for n, w in enumerate(order):
        mine = [p for p in pieces if p[4] == w]
        for p in mine:
            wait(("x", p[0]))
            for i, (op, low, high) in enumerate(emit):
                if op == p[0]:
                    piece = pltpu.make_async_copy(
                        held[op].at[pl.ds(low, high - low)],
                        emitted[i],
                        out_sems.at[nq // tile + 1 + i],
                    )
                    piece.start()
                    sent.append(piece)
        wait(("q", w))
        wait(("v", w))
        last = n == len(order) - 1
        if not last:
            fetch_step(n + 1)
        if last:
            for i in range(len(extra)):
                wait(("e", i))

        def column(low, size, acc, weight, total, lift):
            for op, src, dst, count, _ in mine:
                for m in range(0, count, step):
                    mm = min(step, count - m)
                    at = pl.ds(dst + m, mm)
                    part = jnp.dot(
                        held[op][src + m : src + m + mm],
                        weight[w, :, pl.ds(low, size)],
                        preferred_element_type=jnp.float32,
                    )
                    if last and final:
                        s = held_extra[0][at] + held_extra[1][at].astype(jnp.float32)
                        row = lax.broadcasted_iota(jnp.int32, s.shape, 0) + (dst + m)
                        none = jnp.zeros_like(s)
                        s = jnp.concatenate(
                            [jnp.where(row < bound, s, none), jnp.where(row < bound, none, s)],
                            axis=1,
                        )
                        high = s.astype(jnp.bfloat16)
                        rest = (s - high.astype(jnp.float32)).astype(jnp.bfloat16)
                        for half in (high, rest):
                            part = part + jnp.dot(
                                half, lift[:, pl.ds(low, size)], preferred_element_type=jnp.float32
                            )
                    if any(
                        p[2] <= dst + m and dst + m + mm <= p[2] + p[3]
                        for p in pieces
                        if p[4] in order[:n]
                    ):
                        part = part + acc[at, pl.ds(low, size)]
                    if total is not None:
                        part = part + total[at, pl.ds(low, size)]
                    acc[at, pl.ds(low, size)] = part.astype(acc.dtype)

        nothing = (None, None)
        tq, tv = held_totals if (with_total and last) else nothing
        lq, lv = held_extra[2:] if (final and last) else nothing
        if not last:
            column(0, nq, accs[0], wq, None, None)
        else:

            @pl.loop(0, nq // tile)
            def _(j):
                low = pl.multiple_of(j * tile, tile)
                if with_total:
                    total_tile(j).wait()
                column(low, tile, accs[0], wq, tq, lq)
                at = pl.ds(low, tile)
                pltpu.make_async_copy(
                    accs[0].at[:, at], outs[0].at[:, at], out_sems.at[j]
                ).start()

            if with_total:
                total_value.wait()
        column(0, accs[1].shape[1], accs[1], wv, tv, lv)
    end = pltpu.make_async_copy(accs[1], outs[1], out_sems.at[nq // tile])
    end.start()
    for j in range(nq // tile):
        at = pl.ds(j * tile, tile)
        pltpu.make_async_copy(accs[0].at[:, at], outs[0].at[:, at], out_sems.at[j]).wait()
    end.wait()
    for piece in sent:
        piece.wait()


def matmul(blocks, index, pieces, w_query, w_value, total=None, extra=None, emit=(), tile=TILE, step=STEP):
    weights = 1 + max(p[4] for p in pieces)
    rows = max(p[2] + p[3] for p in pieces)
    width = blocks[0].shape[1]
    nq, nv = w_query.shape[1], w_value.shape[1]
    final = extra is not None
    dtype = jnp.bfloat16 if final else jnp.float32
    operands = list(blocks) + [w_query, w_value]
    scratch = [pltpu.VMEM(b.shape, b.dtype) for b in blocks]
    scratch += [pltpu.VMEM((weights, width, nq), jnp.bfloat16), pltpu.VMEM((weights, width, nv), jnp.bfloat16)]
    if total is not None:
        operands += list(total)
        scratch += [pltpu.VMEM(m.shape, m.dtype) for m in total]
    if final:
        operands += list(extra)
        scratch += [pltpu.VMEM(m.shape, m.dtype) for m in extra]
    scratch += [pltpu.VMEM((rows, nq), dtype), pltpu.VMEM((rows, nv), dtype)]
    copies = len(blocks) + 2 * weights + (4 if final else 0)
    scratch += [pltpu.SemaphoreType.DMA((copies,)), pltpu.SemaphoreType.DMA((nq // tile + 1,))]
    scratch += [pltpu.SemaphoreType.DMA((nq // tile + 1 + len(emit),))]
    hbm = pl.BlockSpec(memory_space=pltpu.HBM)
    in_specs = [hbm] * len(operands)
    flops = 2 * sum(p[3] for p in pieces) * width * (nq + nv)
    moved = sum(o.size * o.dtype.itemsize for o in blocks) + weights * width * (nq + nv) * 2
    moved += rows * (nq + nv) * 4 * (2 if total is not None else 1)
    return pl.pallas_call(
        functools.partial(matmul_kernel, pieces, total is not None, final, emit, tile, step),
        in_specs=[pl.BlockSpec(memory_space=pltpu.SMEM)] + in_specs,
        out_specs=[hbm] * (2 + len(emit)),
        out_shape=[jax.ShapeDtypeStruct((rows, nq), dtype), jax.ShapeDtypeStruct((rows, nv), dtype)]
        + [jax.ShapeDtypeStruct((high - low, width), jnp.bfloat16) for _, low, high in emit],
        scratch_shapes=scratch,
        compiler_params=pltpu.CompilerParams(vmem_limit_bytes=44 * 1024 * 1024),
        cost_estimate=pl.CostEstimate(
            flops=1 if emit else flops, bytes_accessed=1 if emit else moved, transcendentals=0
        ),
    )(index, *operands)


def shrink_kernel(bound, tokens, maps, out, narrow):
    both = jnp.concatenate([maps[0], maps[1]], axis=1)
    sums = jnp.dot(tokens[...], both, preferred_element_type=jnp.float32)
    rank = out.shape[1]
    first = lax.broadcasted_iota(jnp.int32, out.shape, 0) < bound[0]
    out[...] = jnp.where(first, sums[:, :rank], sums[:, rank:])
    narrow[...] = out[...].astype(narrow.dtype)


def partial_shrink(bound, tokens, maps):
    return pl.pallas_call(
        shrink_kernel,
        in_specs=[
            pl.BlockSpec(memory_space=pltpu.SMEM),
            pl.BlockSpec(memory_space=pltpu.VMEM),
            pl.BlockSpec(memory_space=pltpu.VMEM),
        ],
        out_specs=[pl.BlockSpec(memory_space=pltpu.VMEM)] * 2,
        out_shape=[
            jax.ShapeDtypeStruct((tokens.shape[0], maps.shape[2]), jnp.float32),
            jax.ShapeDtypeStruct((tokens.shape[0], maps.shape[2]), jnp.bfloat16),
        ],
        compiler_params=pltpu.CompilerParams(vmem_limit_bytes=24 * 1024 * 1024),
        cost_estimate=pl.CostEstimate(
            flops=4 * tokens.size * maps.shape[2], bytes_accessed=4 << 20, transcendentals=0
        ),
    )(bound, tokens, maps)


def on_device(
    tokens, w_query, w_value, a_both, b_query, b_value, request_adapter, adapter_slot, block_request
):
    rows, width = tokens.shape
    rank = b_query.shape[1]
    mp = lax.axis_index("mp")
    x, z = mp // NZ, mp % NZ
    s = 1 - 2 * (lax.axis_index("dp") % 2)
    bound = (SEG * jnp.sum(block_request[0] == 0)).astype(jnp.int32)

    def place(bx, step):
        return (x ^ bx) * NZ + (z + s * step) % NZ

    def add(blocks, index, pieces, total=None, extra=None, emit=()):
        return matmul(blocks, index, pieces, w_query, w_value, total, extra, emit)

    far, ends, ring = wanted_slots(request_adapter, adapter_slot)
    behind = to_z(tokens, 1)
    ahead = to_z(tokens, -1)
    across = to_x(after(tokens, far))

    other_a = to_core(a_both)
    message = offer(a_both, other_a, after(ends, ring), 4, 4)
    up = to_y(message, 1)
    own_b = jnp.concatenate([after(b_query, message), b_value], axis=2)
    other_b = to_core(own_b)
    total = add([tokens], after(place(0, 0)[None], message, own_b), [(0, 0, 0, rows, 0)])

    ring = after(ring, total[1], other_b)
    down_message = offer(a_both, other_a, ring, 0, 4)
    down = to_y(down_message, -1)
    up_message = offer(a_both, other_a, after(ring, down_message), 4, 4, [(up, 0, 4)])
    up = to_y(up_message, 1)
    first_b_message = offer(own_b, other_b, after(ends, up_message), 4, 4)
    down_b_message = offer(own_b, other_b, after(ring, first_b_message), 0, 4)

    behind = after(behind, down_b_message)
    opposite = to_z(behind, 1)
    cross_message = behind[:EARLY]
    cross_low = to_x(cross_message)
    across = after(across, cross_message)
    across_ahead = to_z(across, -1)

    *total, middle_message, high_message = add(
        [behind],
        after(place(0, -1)[None], cross_message),
        [(0, 0, 0, rows, 0)],
        total,
        emit=((0, EARLY, MIDDLE), (0, MIDDLE, rows)),
    )
    far_message = offer(a_both, other_a, after(ends, total[1]), 2, 2, [(up, 2, 2), (down, 2, 2)])
    far_a = to_far(far_message)
    message = after(first_b_message, far_message)
    up_b = to_y(message, 1)
    total = add(
        [ahead, across],
        after(jnp.stack([place(0, 1), place(1, 0)]), message),
        [(k, 0, 0, rows, k) for k in range(2)],
        total,
    )
    cross_message = after(middle_message, total[1], cross_low)
    cross_middle = to_x(cross_message)
    ends = after(ends, cross_message)

    chosen_a = offer(
        a_both,
        other_a,
        ends,
        0,
        2,
        [(up, 0, 2), (down, 0, 2), (far_a, 0, 2)],
    )
    narrow = lambda v: v.astype(jnp.bfloat16)
    partial, message = partial_shrink(bound[None], tokens, chosen_a)
    half = partial + to_x(message)
    down_b_message = after(down_b_message, message, far_a)
    down_b = to_y(down_b_message, -1)
    ring_b = after(ring, down_b_message)
    up_b_message = offer(own_b, other_b, ring_b, 4, 4, [(up_b, 0, 4)])
    up_b = to_y(up_b_message, 1)

    last_message = after(across_ahead, up_b_message, opposite)
    last = to_z(last_message, -1)
    cross_message = after(high_message, message, cross_middle)
    cross_high = to_x(cross_message)
    message = narrow(half)
    pair = half + to_z(message, 1)
    total = add(
        [opposite],
        after(place(0, 2)[None], cross_message, message),
        [(0, 0, 0, rows, 0)],
        total,
    )
    message = after(narrow(pair), total[1])
    pair_opposite = to_z(message, 2)
    far_b = to_far(
        offer(own_b, other_b, after(ends, message, cross_high), 2, 2, [(up_b, 2, 2), (down_b, 2, 2)])
    )
    total = add(
        [cross_low, cross_middle, cross_high, across_ahead],
        after(jnp.stack([place(1, -1), place(1, 1)]), message),
        [
            (0, 0, 0, EARLY, 0),
            (1, 0, EARLY, MIDDLE - EARLY, 0),
            (2, 0, MIDDLE, rows - MIDDLE, 0),
            (3, 0, 0, rows, 1),
        ],
        total,
    )
    ends = after(ends, total[1])
    wide = offer(
        own_b, other_b, ends, 0, 2, [(up_b, 0, 2), (down_b, 0, 2), (far_b, 0, 2)]
    )
    nq = w_query.shape[1]
    none_q = jnp.zeros((rank, nq), jnp.bfloat16)
    none_v = jnp.zeros((rank, w_value.shape[1]), jnp.bfloat16)
    lift_q = jnp.concatenate([wide[0][:, :nq], none_q, wide[1][:, :nq], none_q])
    lift_v = jnp.concatenate([none_v, wide[0][:, nq:], none_v, wide[1][:, nq:]])

    return tuple(
        add(
            [last],
            jnp.stack([place(1, 2), bound]),
            [(0, 0, 0, rows, 0)],
            total,
            (pair, pair_opposite, lift_q, lift_v),
        )
    )


def solution(mesh):
    placed = (
        P("dp", "mp"),
        P(None, "mp"),
        P(None, "mp"),
        P("dp", "mp", None),
        P("dp", None, "mp"),
        P("dp", None, "mp"),
        P("dp", None),
        P(),
        P("dp", None),
    )
    return jax.shard_map(
        on_device,
        mesh=mesh,
        in_specs=placed,
        out_specs=(P("dp", "mp"), P("dp", "mp")),
        check_vma=False,
    )
```
